32 devices in a mesh: sect: 4 (over z), sec: 8 (over y, x, core).
Axes of the slice: x: 2, y: 2, z: 4, core: 2. Of those that a mesh axis runs over, the one named last changes fastest.
Arguments:
- psi_start: float32 [4, 2048, 32, 400], P('sect', 'sec'), may hold values from -6 to 6
- left_blocks: bfloat16 [4, 3, 1, 2048, 256], P('sect', None, None, 'sec'), may hold values from -0.375 to 0.375
- site_ops: bfloat16 [4, 3, 400, 400], P('sect'), may hold values from -0.3125 to 0.3125
- site_tensors: float32 [4, 256, 20, 32], P('sect', 'sec'), may hold values from -0.5 to 0.5
- env_ops: float32 [4, 3, 20, 20], P('sect'), may hold values from -1.25 to 1.25
- boundary: float32 [3, 256, 32], P(None, 'sec'), may hold values from -6 to 6
- precond: float32 [4, 2048, 32, 400], P('sect', 'sec'), may hold values from 8 to 64
Outputs:
- psi_opt: float32 [4, 2048, 32, 400], P('sect', 'sec')
- energies: float32 [4], P('sect')
The draws below stay inside these ranges and needn't reach their ends.
All inputs are finite; a program needn't handle non-finite values.
Results may differ from the reference program's by a relative error of at most 0.015.
Values may be sent and summed in bfloat16 or wider, within the bound.
A program may use at most 192 MiB of HBM per device.

```python
import math
import jax
import jax.numpy as jnp
from jax import lax

M = 2048
MODALS = 20
RB = 32
KT = 1
ITERS = 4
R_DEV = 256
S = 400
SECTIONS = 4
RT = 256
TERMS = 3
N_SEC = 8


def level_of(key, extent, shards, least, top_value):
    def one(axis_at, parts):
        steps = jax.random.uniform(jax.random.fold_in(jax.random.fold_in(key, 6), axis_at), (parts,), jnp.float32, least / len(shards), top_value / len(shards))
        return jnp.repeat(jnp.exp(steps), extent[axis_at] // parts).reshape((-1,) + (1,) * (len(extent) - axis_at - 1))

    level = one(*shards[0])
    for cut in shards[1:]:
        level = level * one(*cut)
    return level


def normal_values(own_key, extent, width, bound, split=(), dtype=jnp.bfloat16):
    loudness = level_of(own_key, extent, split, -0.22, 0.18) if split else 1.0
    drawn = jax.random.normal(own_key, extent, jnp.float32) * width * loudness
    return jnp.minimum(jnp.maximum(drawn, -bound), bound).astype(dtype)


def setup_inputs(seed: int = 0) -> dict:
    keys = jax.random.split(jax.random.key(seed), 8)
    return {
        "psi_start": normal_values(keys[0], (SECTIONS, M, RB, S), 1.0, 6.0, ((0, 4), (1, 8)), jnp.float32),
        "left_blocks": normal_values(keys[1], (SECTIONS, 3, KT, M, R_DEV), R_DEV ** -0.5, 0.375, ((0, 4), (3, 8))),
        "site_ops": normal_values(keys[2], (SECTIONS, TERMS, S, S), S ** -0.5, 0.3125, ((0, 4),)),
        "site_tensors": normal_values(keys[3], (SECTIONS, RT, MODALS, RB), (RB * (MODALS + 12) // 8) ** -0.5, 0.5, ((0, 4), (1, 8)), jnp.float32),
        "env_ops": normal_values(keys[4], (SECTIONS, TERMS, MODALS, MODALS), MODALS ** -0.5, 1.25, ((0, 4),), jnp.float32),
        "boundary": normal_values(keys[5], (TERMS, RT, RB), 1.0, 6.0, ((1, 8),), jnp.float32),
        "precond": jnp.clip(jnp.exp(math.log(64.0) - 2.0794415 * jax.random.uniform(keys[6], (SECTIONS, M, RB, S), jnp.float32) ** level_of(keys[6], (SECTIONS, M, RB, S), ((0, 4), (1, 8)), -0.2, 0.2)), 8.0, 64.0),
    }


def advance(tensors, operators, environ):
    highest = lax.Precision.HIGHEST
    first = jnp.einsum('qcpx,kqxy->kqcpy', tensors, environ, precision=highest)
    second = jnp.einsum('kqcpy,kpz->kqczy', first, operators, precision=highest)
    return jnp.einsum('kqczy,qbzy->kqcb', second, tensors, precision=highest)

def reference(psi_start, left_blocks, site_ops, site_tensors, env_ops, boundary, precond):
    sections = psi_start.shape[0]
    row_dev = M // N_SEC
    block_count = M // row_dev
    bond_size = psi_start.shape[2]
    pair_count = psi_start.shape[3]
    term_count = boundary.shape[0]
    environs = [None] * sections
    current = boundary.reshape(term_count, block_count, bond_size, bond_size)
    for section in reversed(range(sections)):
        tensors = site_tensors[section].reshape(block_count, bond_size, MODALS, bond_size)
        current = advance(tensors, env_ops[section], current)
        environs[section] = current
    results = []
    energy_list = []
    for section in range(sections):
        lowered_env = lax.optimization_barrier(environs[section].astype(jnp.bfloat16)).astype(jnp.float32)
        environ = lowered_env.reshape(3, KT, block_count, bond_size, bond_size)
        operators = site_ops[section].reshape(3, KT, pair_count, pair_count).astype(jnp.float32)
        couplings = left_blocks[section].reshape(3, KT, block_count, row_dev, row_dev).astype(jnp.float32)
        inverse = 1.0 / precond[section]
        vector = psi_start[section]
        ritz_value = jnp.float32(0.0)
        for iteration in range(ITERS):
            lowered = vector.astype(jnp.bfloat16)
            lowered = lax.optimization_barrier(lowered).astype(jnp.float32)
            blocks = lowered.reshape(block_count, row_dev, bond_size, pair_count)
            padded = jnp.pad(blocks, ((1, 1), (0, 0), (0, 0), (0, 0)))
            image = jnp.zeros((block_count, row_dev, bond_size, pair_count), jnp.float32)
            for position in range(3):
                nearby = padded[position:position + block_count]
                factors = jnp.einsum('kqrj,qjbs->kqrbs', couplings[position], nearby)
                factors = lax.optimization_barrier(factors.astype(jnp.bfloat16)).astype(jnp.float32)
                mixed = jnp.einsum('kqrbs,kts->kqrbt', factors, operators[position])
                mixed = lax.optimization_barrier(mixed.astype(jnp.bfloat16)).astype(jnp.float32)
                image = image + jnp.einsum('kqcb,kqrbt->qrct', environ[position], mixed, precision=lax.Precision.HIGHEST)
            image = image.reshape(vector.shape)
            ritz_value = jnp.sum(vector * image) / jnp.sum(vector * vector)
            updated = vector - (image - ritz_value * vector) * inverse
            vector = updated * lax.rsqrt(jnp.mean(updated * updated) + 1e-06)
        results.append(vector)
        energy_list.append(ritz_value)
    return (jnp.stack(results), jnp.stack(energy_list))
```

```python
import functools
import jax
import jax.numpy as jnp
from jax import lax
from jax.experimental import pallas as pl
from jax.experimental.pallas import tpu as pltpu
from jax.sharding import PartitionSpec as P

ITERS = 4
STATES = 4


def from_behind(shard, axis, by):
    count = lax.axis_size(axis)
    pairs = [(i, i + by) for i in range(count) if 0 <= i + by < count]
    return lax.ppermute(shard, axis, pairs)


def couple_and_mix(part_ref, coupling_ref, operator_ref, out_ref):
    coupling = coupling_ref[0]
    operator = operator_ref[0]
    for at in range(part_ref.shape[0]):
        u = lax.dot_general(
            part_ref[at], coupling, (((1,), (1,)), ((), ())), preferred_element_type=jnp.float32
        ).astype(jnp.bfloat16)
        out_ref[0, at] = jnp.dot(operator, u, preferred_element_type=jnp.float32).astype(
            jnp.bfloat16
        )


def own_block(lowered, couplings, operators):
    bond_size, pair_count, row_count = lowered.shape
    flops = 2 * bond_size * pair_count * row_count * (row_count + pair_count)
    return pl.pallas_call(
        couple_and_mix,
        out_shape=jax.ShapeDtypeStruct((3,) + lowered.shape, jnp.bfloat16),
        grid=(bond_size // STATES,),
        in_specs=[
            pl.BlockSpec((STATES, pair_count, row_count), lambda i: (i, 0, 0)),
            pl.BlockSpec((1, row_count, row_count), lambda i: (1, 0, 0)),
            pl.BlockSpec((1, pair_count, pair_count), lambda i: (1, 0, 0)),
        ],
        out_specs=pl.BlockSpec((1, STATES, pair_count, row_count), lambda i: (1, i, 0, 0)),
        compiler_params=pltpu.CompilerParams(vmem_limit_bytes=32 * 2**20),
        cost_estimate=pl.CostEstimate(
            flops=flops, bytes_accessed=4 * lowered.size, transcendentals=0
        ),
    )(lowered, couplings, operators)


def side_kernel(half, relay, detour_ref, *refs):
    parts, (coupling_ref, operator_ref, _, out_ref) = refs[:-4], refs[-4:]
    side, step = pl.program_id(0), pl.program_id(1)
    other = detour_ref[side] == 1
    run = lambda ref: couple_and_mix(ref, coupling_ref, operator_ref, out_ref)
    straight = jnp.logical_not(other)
    pl.when(jnp.logical_and(straight, side == 0))(lambda: run(parts[0]))
    pl.when(jnp.logical_and(straight, side == 1))(lambda: run(parts[1]))
    if relay:
        pl.when(jnp.logical_and(other, step < half))(lambda: run(parts[2]))
        pl.when(jnp.logical_and(other, step >= half))(lambda: run(parts[3]))


def side_blocks(detour, parts, couplings, operators, mixed):
    bond_size, pair_count, row_count = mixed.shape[1:]
    steps = bond_size // STATES
    half = steps // 2
    relay = len(parts) == 4
    block = (STATES, pair_count, row_count)

    def low(k, i, detour_ref):
        return (jnp.where((k == 0) & (detour_ref[0] == 0), i, steps - 1), 0, 0)

    def high(k, i, detour_ref):
        return (jnp.where((k == 1) & (detour_ref[1] == 0), i, 0), 0, 0)

    def first(k, i, detour_ref):
        return (jnp.where(detour_ref[k] == 1, jnp.minimum(i, half - 1), 0), 0, 0)

    def second(k, i, detour_ref):
        return (jnp.where(detour_ref[k] == 1, jnp.maximum(i - half, 0), 0), 0, 0)

    maps = [low, high, first, second][: len(parts)]
    flops = 4 * bond_size * pair_count * row_count * (row_count + pair_count)
    return pl.pallas_call(
        functools.partial(side_kernel, half, relay),
        out_shape=jax.ShapeDtypeStruct(mixed.shape, mixed.dtype),
        grid_spec=pltpu.PrefetchScalarGridSpec(
            num_scalar_prefetch=1,
            grid=(2, steps),
            in_specs=[pl.BlockSpec(block, at) for at in maps]
            + [
                pl.BlockSpec((1, row_count, row_count), lambda k, i, d: (2 * k, 0, 0)),
                pl.BlockSpec((1, pair_count, pair_count), lambda k, i, d: (2 * k, 0, 0)),
                pl.BlockSpec(memory_space=pl.ANY),
            ],
            out_specs=pl.BlockSpec((1,) + block, lambda k, i, d: (2 * k, i, 0, 0)),
        ),
        input_output_aliases={len(parts) + 3: 0},
        compiler_params=pltpu.CompilerParams(vmem_limit_bytes=32 * 2**20),
        cost_estimate=pl.CostEstimate(
            flops=flops, bytes_accessed=8 * bond_size * pair_count * row_count, transcendentals=0
        ),
    )(detour, *parts, couplings, operators, mixed)


def exchange(lowered, place):
    count = lax.axis_size("sec")
    forward = [(i, i + 1) for i in range(count - 1)]
    if count != 8:
        low = lax.ppermute(lowered, "sec", forward)
        high = lax.ppermute(lowered, "sec", [(b, a) for a, b in forward])
        return [low, high], jnp.zeros((2,), jnp.int32)
    half = lowered.shape[0] // 2
    leg = lax.ppermute(lowered[:half], "sec", [(3, 7), (4, 0)])
    straight = lax.ppermute(lowered[half:], "sec", [(3, 4), (4, 3)])
    forward.remove((3, 4))
    low = lax.ppermute(lowered, "sec", forward)
    high = lax.ppermute(lowered, "sec", [(b, a) for a, b in forward])
    round_by = lax.ppermute(leg, "sec", [(7, 4), (0, 3)])
    detour = jnp.stack([place == 4, place == 3]).astype(jnp.int32)
    return [low, high, round_by, straight], detour


def advance(tensors, operators, environ):
    highest = lax.Precision.HIGHEST
    first = jnp.einsum("cpx,kxy->kcpy", tensors, environ, precision=highest)
    second = jnp.einsum("kcpy,kpz->kczy", first, operators, precision=highest)
    return jnp.einsum("kczy,bzy->kcb", second, tensors, precision=highest)


def on_device(psi_start, left_blocks, site_ops, site_tensors, env_ops, boundary, precond):
    tensors_here = site_tensors[0]
    operators_here = env_ops[0]
    position_sect = lax.axis_index("sect")
    place = lax.axis_index("sec")
    final_sect = lax.axis_size("sect") - 1
    current = advance(tensors_here, operators_here, boundary)
    for step in range(lax.axis_size("sect") - 1):
        received = from_behind(current, "sect", -1)
        current = jnp.where(
            position_sect == final_sect, current, advance(tensors_here, operators_here, received)
        )
    kept = jnp.transpose(psi_start[0], (1, 2, 0))
    inverse = 1.0 / jnp.transpose(precond[0], (1, 2, 0))
    environ = current.astype(jnp.bfloat16)
    operators = site_ops[0]
    couplings = left_blocks[0, :, 0]
    cell_count = kept.size * lax.axis_size("sec")
    ritz_value = jnp.float32(0.0)
    scale = jnp.float32(1.0)
    lowered = kept.astype(jnp.bfloat16)
    for iteration in range(ITERS):
        parts, detour = exchange(lowered, place)
        mixed = own_block(lowered, couplings, operators)
        mixed = side_blocks(detour, parts, couplings, operators, mixed)
        image = jnp.einsum("kcb,kbtr->ctr", environ, mixed, preferred_element_type=jnp.float32)
        small = image * (1.0 / 64.0)
        intersection, norm_sq, size = lax.psum(
            (jnp.sum(kept * image), jnp.sum(kept * kept), jnp.sum(small * small)), "sec"
        )
        if iteration:
            scale = scale * lax.rsqrt(scale * scale * (norm_sq / cell_count) + 1e-06)
        ritz_value = intersection / norm_sq
        factor = lax.rsqrt((norm_sq + size) / cell_count)
        kept = (kept - (image - ritz_value * kept) * inverse) * factor
        lowered = kept.astype(jnp.bfloat16)
        scale = scale / factor
    norm_sq = lax.psum(jnp.sum(kept * kept), "sec")
    scale = scale * lax.rsqrt(scale * scale * (norm_sq / cell_count) + 1e-06)
    vector = jnp.transpose(kept * scale, (2, 0, 1))
    return (vector[None], jnp.reshape(ritz_value, (1,)))


def solution(mesh):
    placed = (
        P("sect", "sec", None, None),
        P("sect", None, None, "sec", None),
        P("sect", None, None, None),
        P("sect", "sec", None, None),
        P("sect", None, None, None),
        P(None, "sec", None),
        P("sect", "sec", None, None),
    )
    return jax.shard_map(
        on_device,
        mesh=mesh,
        in_specs=placed,
        out_specs=(P("sect", "sec", None, None), P("sect")),
        check_vma=False,
    )
```

```python
import functools
import jax
import jax.numpy as jnp
from jax import lax
from jax.experimental import pallas as pl
from jax.experimental.pallas import tpu as pltpu
from jax.sharding import PartitionSpec as P

ITERS = 4
STATES = 4


def from_behind(shard, axis, by):
    count = lax.axis_size(axis)
    pairs = [(i, i + by) for i in range(count) if 0 <= i + by < count]
    return lax.ppermute(shard, axis, pairs)


def couple_and_mix(part_ref, coupling_ref, operator_ref, out_ref):
    coupling = coupling_ref[0]
    operator = operator_ref[0]
    for at in range(part_ref.shape[0]):
        u = lax.dot_general(
            part_ref[at], coupling, (((1,), (1,)), ((), ())), preferred_element_type=jnp.float32
        ).astype(jnp.bfloat16)
        out_ref[0, at] = jnp.dot(operator, u, preferred_element_type=jnp.float32).astype(
            jnp.bfloat16
        )


def own_block(lowered, couplings, operators):
    bond_size, pair_count, row_count = lowered.shape
    flops = 2 * bond_size * pair_count * row_count * (row_count + pair_count)
    return pl.pallas_call(
        couple_and_mix,
        out_shape=jax.ShapeDtypeStruct((3,) + lowered.shape, jnp.bfloat16),
        grid=(bond_size // STATES,),
        in_specs=[
            pl.BlockSpec((STATES, pair_count, row_count), lambda i: (i, 0, 0)),
            pl.BlockSpec((1, row_count, row_count), lambda i: (1, 0, 0)),
            pl.BlockSpec((1, pair_count, pair_count), lambda i: (1, 0, 0)),
        ],
        out_specs=pl.BlockSpec((1, STATES, pair_count, row_count), lambda i: (1, i, 0, 0)),
        compiler_params=pltpu.CompilerParams(vmem_limit_bytes=32 * 2**20),
        cost_estimate=pl.CostEstimate(
            flops=flops, bytes_accessed=4 * lowered.size, transcendentals=0
        ),
    )(lowered, couplings, operators)


def side_kernel(half, relay, detour_ref, *refs):
    parts, (coupling_ref, operator_ref, _, out_ref) = refs[:-4], refs[-4:]
    side, step = pl.program_id(0), pl.program_id(1)
    other = detour_ref[side] == 1
    run = lambda ref: couple_and_mix(ref, coupling_ref, operator_ref, out_ref)
    straight = jnp.logical_not(other)
    pl.when(jnp.logical_and(straight, side == 0))(lambda: run(parts[0]))
    pl.when(jnp.logical_and(straight, side == 1))(lambda: run(parts[1]))
    if relay:
        pl.when(jnp.logical_and(other, step < half))(lambda: run(parts[2]))
        pl.when(jnp.logical_and(other, step >= half))(lambda: run(parts[3]))


def side_blocks(detour, parts, couplings, operators, mixed):
    bond_size, pair_count, row_count = mixed.shape[1:]
    steps = bond_size // STATES
    half = steps // 2
    relay = len(parts) == 4
    block = (STATES, pair_count, row_count)

    def low(k, i, detour_ref):
        return (jnp.where((k == 0) & (detour_ref[0] == 0), i, steps - 1), 0, 0)

    def high(k, i, detour_ref):
        return (jnp.where((k == 1) & (detour_ref[1] == 0), i, 0), 0, 0)

    def first(k, i, detour_ref):
        return (jnp.where(detour_ref[k] == 1, jnp.minimum(i, half - 1), 0), 0, 0)

    def second(k, i, detour_ref):
        return (jnp.where(detour_ref[k] == 1, jnp.maximum(i - half, 0), 0), 0, 0)

    maps = [low, high, first, second][: len(parts)]
    flops = 4 * bond_size * pair_count * row_count * (row_count + pair_count)
    return pl.pallas_call(
        functools.partial(side_kernel, half, relay),
        out_shape=jax.ShapeDtypeStruct(mixed.shape, mixed.dtype),
        grid_spec=pltpu.PrefetchScalarGridSpec(
            num_scalar_prefetch=1,
            grid=(2, steps),
            in_specs=[pl.BlockSpec(block, at) for at in maps]
            + [
                pl.BlockSpec((1, row_count, row_count), lambda k, i, d: (2 * k, 0, 0)),
                pl.BlockSpec((1, pair_count, pair_count), lambda k, i, d: (2 * k, 0, 0)),
                pl.BlockSpec(memory_space=pl.ANY),
            ],
            out_specs=pl.BlockSpec((1,) + block, lambda k, i, d: (2 * k, i, 0, 0)),
        ),
        input_output_aliases={len(parts) + 3: 0},
        compiler_params=pltpu.CompilerParams(vmem_limit_bytes=32 * 2**20),
        cost_estimate=pl.CostEstimate(
            flops=flops, bytes_accessed=8 * bond_size * pair_count * row_count, transcendentals=0
        ),
    )(detour, *parts, couplings, operators, mixed)


def exchange(lowered, place):
    count = lax.axis_size("sec")
    forward = [(i, i + 1) for i in range(count - 1)]
    if count != 8:
        low = lax.ppermute(lowered, "sec", forward)
        high = lax.ppermute(lowered, "sec", [(b, a) for a, b in forward])
        return [low, high], jnp.zeros((2,), jnp.int32)
    half = lowered.shape[0] // 2
    leg = lax.ppermute(lowered[:half], "sec", [(3, 7), (4, 0)])
    straight = lax.ppermute(lowered[half:], "sec", [(3, 4), (4, 3)])
    forward.remove((3, 4))
    low = lax.ppermute(lowered, "sec", forward)
    high = lax.ppermute(lowered, "sec", [(b, a) for a, b in forward])
    round_by = lax.ppermute(leg, "sec", [(7, 4), (0, 3)])
    detour = jnp.stack([place == 4, place == 3]).astype(jnp.int32)
    return [low, high, round_by, straight], detour


def advance(tensors, operators, environ):
    highest = lax.Precision.HIGHEST
    first = jnp.einsum("cpx,kxy->kcpy", tensors, environ, precision=highest)
    second = jnp.einsum("kcpy,kpz->kczy", first, operators, precision=highest)
    return jnp.einsum("kczy,bzy->kcb", second, tensors, precision=highest)


def on_device(psi_start, left_blocks, site_ops, site_tensors, env_ops, boundary, precond):
    tensors_here = site_tensors[0]
    operators_here = env_ops[0]
    position_sect = lax.axis_index("sect")
    place = lax.axis_index("sec")
    final_sect = lax.axis_size("sect") - 1
    current = advance(tensors_here, operators_here, boundary)
    for step in range(lax.axis_size("sect") - 1):
        received = from_behind(current, "sect", -1)
        current = jnp.where(
            position_sect == final_sect, current, advance(tensors_here, operators_here, received)
        )
    kept = jnp.transpose(psi_start[0], (1, 2, 0))
    inverse = 1.0 / jnp.transpose(precond[0], (1, 2, 0))
    environ = current.astype(jnp.bfloat16)
    operators = site_ops[0]
    couplings = left_blocks[0, :, 0]
    cell_count = kept.size * lax.axis_size("sec")
    ritz_value = jnp.float32(0.0)
    scale = jnp.float32(1.0)
    lowered = kept.astype(jnp.bfloat16)
    for iteration in range(ITERS):
        parts, detour = exchange(lowered, place)
        mixed = own_block(lowered, couplings, operators)
        mixed = side_blocks(detour, parts, couplings, operators, mixed)
        image = jnp.einsum("kcb,kbtr->ctr", environ, mixed, preferred_element_type=jnp.float32)
        small = image * (1.0 / 64.0)
        intersection, norm_sq, size = lax.psum(
            (jnp.sum(kept * image), jnp.sum(kept * kept), jnp.sum(small * small)), "sec"
        )
        if iteration:
            scale = scale * lax.rsqrt(scale * scale * (norm_sq / cell_count) + 1e-06)
        ritz_value = intersection / norm_sq
        factor = lax.rsqrt((norm_sq + size) / cell_count)
        kept = (kept - (image - ritz_value * kept) * inverse) * factor
        lowered = kept.astype(jnp.bfloat16)
        scale = scale / factor
    kept, local_sq = lax.optimization_barrier((kept, jnp.sum(kept * kept)))
    norm_sq = lax.psum(local_sq, "sec")
    scale = scale * lax.rsqrt(scale * scale * (norm_sq / cell_count) + 1e-06)
    vector = jnp.transpose(kept * scale, (2, 0, 1))
    return (vector[None], jnp.reshape(ritz_value, (1,)))


def solution(mesh):
    placed = (
        P("sect", "sec", None, None),
        P("sect", None, None, "sec", None),
        P("sect", None, None, None),
        P("sect", "sec", None, None),
        P("sect", None, None, None),
        P(None, "sec", None),
        P("sect", "sec", None, None),
    )
    return jax.shard_map(
        on_device,
        mesh=mesh,
        in_specs=placed,
        out_specs=(P("sect", "sec", None, None), P("sect")),
        check_vma=False,
    )
```
